256 devices in a mesh: section: 2 (over y_hi), fsdp: 64 (over y_lo, x, z), mp: 2 (over core).
Axes of the slice: x: 4, y: 4 (y_hi: 2, y_lo: 2; y = y_hi * 2 + y_lo), z: 8, core: 2. Of those that a mesh axis runs over, the one named last changes fastest.
Arguments:
- section_rows: bfloat16 [2, 8192, 4096], P('section', 'fsdp', 'mp'), may hold values from -6 to 6
- norm_gains: bfloat16 [2, 4096], P('section', 'mp'), may hold values from 0.5 to 1.5
- proj_weights: bfloat16 [2, 4096, 2, 2048], P('section', 'fsdp', None, 'mp'), may hold values from -1 to 1
- section_cotan: bfloat16 [2, 8192, 4096], P('section', 'fsdp', 'mp'), may hold values from -6 to 6
- enc_lengths: int32 [64, 2], P('fsdp'), may hold values from 1 to 64, 96 in all within a row
- dec_segments: int32 [64, 128], P('fsdp'), may hold values from 0 to 1, never falling along the last dimension, each value on 1 to 127 neighbouring positions
Outputs:
- section_grads: float32 [2, 8192, 4096], P('section', 'fsdp', 'mp')
The draws below stay inside these ranges and needn't reach their ends.
Inputs may be any that keep to these rules, and one draw needn't show every extreme that they name: `enc_lengths`: each row of an fsdp index sums to 96. `dec_segments`: never falls along a row; each slot owns 1 to 127 rows.
All inputs are finite; a program needn't handle non-finite values.
Results may differ from the reference program's by a relative error of at most 0.024.
Values may be sent and summed in bfloat16 or wider, within the bound.
No kernel may reach another device: no remote copies, remote signals or barrier semaphores. Data moves between devices by JAX's collectives and lax.ppermute only.
A program may use at most 64 MiB of HBM per device.

```python
import math
import jax
import jax.numpy as jnp
import numpy as np
from jax import lax

D = 4096
HD = 64
ELEN = 64
SEQUENCES_SHARD = 2
INNER = 2048
ROWS = 128
NR = 8192
N_FSDP = 64


def draw_section_rows(key, part):
    key = jax.random.fold_in(key, 1)
    noise_key = jax.random.fold_in(key, 0)
    all_rows = jax.random.normal(noise_key, (2, NR, D), jnp.float32)
    return jnp.clip(all_rows, -6.0, 6.0).astype(jnp.bfloat16)


def draw_proj_weights(key, part):
    key = jax.random.fold_in(key, 2)
    noise_key = jax.random.fold_in(key, 0)
    spread = jnp.array([[1.0, 1.0], [HD ** (-0.5), 1.0]], jnp.float32)[:, None, :, None] * D ** (-0.5)
    weight_tensors = jnp.clip(jax.random.normal(noise_key, (2, D, 2, INNER), jnp.float32), -6.0, 6.0) * spread
    return jnp.clip(weight_tensors, -1.0, 1.0).astype(jnp.bfloat16)


def shard_levels(own_key, shape, cuts, low, high):
    level, own = 1.0, jax.random.fold_in(own_key, 6)
    for axis_at, blocks in cuts:
        steps = jnp.exp(jax.random.uniform(jax.random.fold_in(own, axis_at), (blocks,), jnp.float32, low / len(cuts), high / len(cuts)))
        level = level * jnp.repeat(steps, shape[axis_at] // blocks).reshape([-1 if axis == axis_at else 1 for axis in range(len(shape))])
    return level


def profile(count, total, limit, skew):
    portions = [(1 << 20) // math.isqrt(rank ** skew) + 1 for rank in range(2, count + 1)]
    spare, given = total - limit - (count - 1), [1] * (count - 1)
    while spare > 0:
        candidates = [i for i in range(count - 1) if given[i] < limit]
        pool, remaining = sum([portions[i] for i in candidates]), spare
        for i in candidates:
            addition = min(limit - given[i], max(1, remaining * portions[i] // pool), spare)
            given[i] = given[i] + addition
            spare = spare - addition
    return np.array([limit] + given)


def uneven(own_key, count, total, most, lean):
    if count == 2:
        one = jax.random.randint(own_key, (), max(1, total - most), min(most, total - 1) + 1)
        return jnp.stack([one, total - one])
    sizes = jnp.asarray(profile(count, total, most, lean), jnp.int32)
    couples = (count - 1) // 2
    donor, receiver = sizes[1:1 + 2 * couples:2], sizes[2:2 + 2 * couples:2]
    margin = jnp.minimum(donor - 1, most - receiver)
    moved = jax.random.randint(jax.random.fold_in(own_key, 1), (couples,), 0, 1 << 20) % (margin + 1)
    sizes = sizes.at[1:1 + 2 * couples:2].set(donor - moved).at[2:2 + 2 * couples:2].set(receiver + moved)
    return sizes[jax.random.permutation(jax.random.fold_in(own_key, 2), count)]


def gaussian(own_key, extent, width, most, shards=(), dtype=jnp.bfloat16):
    entries = jax.random.normal(own_key, extent, jnp.float32) * width
    if len(shards) > 0:
        entries = shard_levels(own_key, extent, shards, -0.22, 0.18) * entries
    return jnp.clip(entries, min=-most, max=most).astype(dtype)


def setup_inputs(seed: int = 0) -> dict:
    seeds = jax.random.split(jax.random.key(seed), 7)
    section_rows = draw_section_rows(jax.random.fold_in(seeds[6], 71), 0)
    norm_gains = jnp.clip(1.0 + 0.1 * jax.random.normal(seeds[1], (2, D), jnp.float32), 0.5, 1.5).astype(jnp.bfloat16)
    proj_weights = draw_proj_weights(jax.random.fold_in(seeds[6], 71), 0)
    section_cotan = gaussian(seeds[3], (2, NR, D), 1.0, 6.0, ((0, 2), (1, 64), (2, 2)))
    enc_lengths = jax.vmap(lambda own: uneven(own, SEQUENCES_SHARD, SEQUENCES_SHARD * ELEN * 3 // 4, ELEN, 2))(jax.random.split(seeds[4], N_FSDP)).reshape((N_FSDP, SEQUENCES_SHARD)).astype(jnp.int32)
    dec_segments = jax.vmap(lambda own: jnp.searchsorted(jnp.cumsum(uneven(own, SEQUENCES_SHARD, ROWS, 2 * ELEN - 1, 1)), jnp.arange(ROWS), side="right"))(jax.random.split(seeds[5], N_FSDP)).reshape((N_FSDP, ROWS)).astype(jnp.int32)
    return dict(section_rows=section_rows, norm_gains=norm_gains, proj_weights=proj_weights, section_cotan=section_cotan, enc_lengths=enc_lengths, dec_segments=dec_segments)


EPS = 1e-06

def normalize(rows, gain_row):
    wide_rows = rows.astype(jnp.float32)
    inverse = lax.rsqrt(lax.optimization_barrier(jnp.mean(wide_rows * wide_rows, -1, keepdims=True)) + EPS)
    normed = (wide_rows * inverse * gain_row.astype(jnp.float32)).astype(jnp.bfloat16)
    return (wide_rows, inverse, normed)

def norm_grad(wide_rows, inverse, gain_row, upstream):
    gain_grad = gain_row.astype(jnp.float32) * upstream
    row_dot = lax.optimization_barrier(jnp.mean(wide_rows * gain_grad, -1, keepdims=True))
    return inverse * gain_grad - wide_rows * inverse ** 3 * row_dot

def attention_grads(query, output_grad, keys, values, segment, lengths):
    row_count = query.shape[0]
    head_count = query.shape[1] // HD
    key_index = jnp.arange(row_count)
    key_seq = key_index // ELEN
    slot_ids = jnp.arange(lengths.shape[0])
    key_len = lax.optimization_barrier(jnp.sum(jnp.where(key_seq[:, None] == slot_ids[None, :], lengths[None, :], 0), 1))
    allowed = (segment[:, None] == key_seq[None, :]) & (key_index % ELEN < key_len)[None, :]
    head_shape = (row_count, head_count, HD)
    query_heads = query.reshape(head_shape).astype(jnp.float32)
    key_heads = keys.reshape(head_shape).astype(jnp.float32)
    value_heads = values.reshape(head_shape).astype(jnp.float32)
    grad_heads = output_grad.reshape(head_shape).astype(jnp.float32)
    scores = jnp.einsum('qhd,khd->hqk', query_heads, key_heads)
    scores = jnp.where(allowed[None], scores, -1e+30)
    row_peak = lax.optimization_barrier(jnp.max(scores, -1, keepdims=True))
    exponent = jnp.exp(scores - row_peak)
    softmax_rows = exponent / lax.optimization_barrier(jnp.sum(exponent, -1, keepdims=True))
    soft_low = softmax_rows.astype(jnp.bfloat16)
    attended = jnp.einsum('hqk,khd->qhd', soft_low.astype(jnp.float32), value_heads).astype(jnp.bfloat16)
    row_delta = lax.optimization_barrier(jnp.sum(grad_heads * attended.astype(jnp.float32), -1))
    prob_grad = jnp.einsum('qhd,khd->hqk', grad_heads, value_heads)
    score_grad = (softmax_rows * (prob_grad - jnp.transpose(row_delta)[:, :, None])).astype(jnp.bfloat16)
    score_wide = score_grad.astype(jnp.float32)
    query_grad = jnp.einsum('hqk,khd->qhd', score_wide, key_heads).astype(jnp.bfloat16)
    key_grad = jnp.einsum('hqk,qhd->khd', score_wide, query_heads).astype(jnp.bfloat16)
    value_grad = jnp.einsum('hqk,qhd->khd', soft_low.astype(jnp.float32), grad_heads).astype(jnp.bfloat16)
    flat = (row_count, head_count * HD)
    return (query_grad.reshape(flat), key_grad.reshape(flat), value_grad.reshape(flat))

def reference(section_rows, norm_gains, proj_weights, section_cotan, enc_lengths, dec_segments):
    block_rows = SEQUENCES_SHARD * ELEN
    enc_weights = proj_weights[0]
    dec_weights = proj_weights[1]

    def per_block(pieces):
        enc_block, decoder_block, enc_cot, dec_cot, lengths, segment = pieces
        enc_wide, enc_inverse, enc_normed = normalize(enc_block, norm_gains[0])
        dec_wide, dec_inverse, dec_normed = normalize(decoder_block, norm_gains[1])
        keys = jnp.dot(enc_normed, enc_weights[:, 0], preferred_element_type=jnp.float32).astype(jnp.bfloat16)
        values = jnp.dot(enc_normed, enc_weights[:, 1], preferred_element_type=jnp.float32).astype(jnp.bfloat16)
        query = jnp.dot(dec_normed, dec_weights[:, 0], preferred_element_type=jnp.float32).astype(jnp.bfloat16)
        output_grad = jnp.dot(dec_cot, dec_weights[:, 1], preferred_element_type=jnp.float32).astype(jnp.bfloat16)
        query_grad, key_grad, value_grad = attention_grads(query, output_grad, keys, values, segment, lengths)
        enc_up = jnp.dot(key_grad, enc_weights[:, 0].T, preferred_element_type=jnp.float32)
        enc_up = enc_up + jnp.dot(value_grad, enc_weights[:, 1].T, preferred_element_type=jnp.float32)
        enc_up = enc_up + enc_cot.astype(jnp.float32)
        dec_up = jnp.dot(query_grad, dec_weights[:, 0].T, preferred_element_type=jnp.float32)
        enc_grad = norm_grad(enc_wide, enc_inverse, norm_gains[0], enc_up)
        dec_grad = norm_grad(dec_wide, dec_inverse, norm_gains[1], dec_up) + dec_cot.astype(jnp.float32)
        return (enc_grad, dec_grad)
    inputs = (section_rows[0].reshape(N_FSDP, block_rows, D), section_rows[1].reshape(N_FSDP, block_rows, D), section_cotan[0].reshape(N_FSDP, block_rows, D), section_cotan[1].reshape(N_FSDP, block_rows, D), enc_lengths, dec_segments)
    enc_grads, dec_grads = lax.map(per_block, inputs)
    return jnp.stack((enc_grads.reshape(-1, D), dec_grads.reshape(-1, D)))
```

```python
import jax
import jax.numpy as jnp
import numpy as np
from jax import lax
from jax.experimental import pallas as pl
from jax.experimental.pallas import tpu as pltpu
from jax.sharding import Mesh, PartitionSpec as P

HD = 64
ELEN = 64
EPS = 1e-06
BF = jnp.bfloat16
F32 = jnp.float32


def shift(block, axis, distance):
    size = lax.axis_size(axis)
    return lax.ppermute(block, axis, [(i, (i + distance) % size) for i in range(size)])


def dot(left, right, contract):
    return lax.dot_general(left, right, (contract, ((), ())), preferred_element_type=F32)


def attention_kernel(lengths_ref, side_ref, keep_ref, recv_ref, segment_ref, stay_ref, send_ref):
    at_encoder = side_ref[0] == 0
    rows = segment_ref.shape[1]
    key_index = lax.broadcasted_iota(jnp.int32, (rows, rows), 1)
    lane = lax.broadcasted_iota(jnp.int32, (rows, 2 * HD), 1)
    slot = key_index // ELEN
    place = key_index % ELEN
    for block in range(segment_ref.shape[0]):
        pick = pl.ds(block * rows, rows)
        kept = [keep_ref[part, pick, :] for part in range(2)]
        received = [recv_ref[part, pick, :] for part in range(2)]
        query, output_grad = [jnp.where(at_encoder, r, k) for k, r in zip(kept, received)]
        keys, values = [jnp.where(at_encoder, k, r) for k, r in zip(kept, received)]
        key_len = jnp.where(slot == 0, lengths_ref[block, 0], lengths_ref[block, 1])
        allowed = (segment_ref[block] == slot) & (place < key_len)
        sums = None
        for head in range(2):
            mine = lane // HD == head
            query_head = jnp.where(mine, query, 0)
            grad_head = jnp.where(mine, output_grad, 0)
            scores = dot(query_head, keys, ((1,), (1,)))
            scores = jnp.where(allowed, scores, -1e30)
            exponent = jnp.exp(scores - jnp.max(scores, -1, keepdims=True))
            softmax_rows = exponent / jnp.sum(exponent, -1, keepdims=True)
            soft_low = softmax_rows.astype(BF)
            attended = dot(soft_low, values, ((1,), (0,))).astype(BF)
            row_delta = jnp.sum(grad_head.astype(F32) * attended.astype(F32), -1, keepdims=True)
            prob_grad = dot(grad_head, values, ((1,), (1,)))
            score_grad = (softmax_rows * (prob_grad - row_delta)).astype(BF)
            query_grad = dot(score_grad, keys, ((1,), (0,)))
            key_grad = dot(score_grad, query, ((0,), (0,)))
            value_grad = dot(soft_low, output_grad, ((0,), (0,)))
            grads = (query_grad, key_grad, value_grad)
            sums = grads if head == 0 else [jnp.where(mine, g, s) for g, s in zip(grads, sums)]
        query_grad, key_grad, value_grad = [g.astype(BF) for g in sums]
        empty = jnp.zeros_like(query_grad)
        stay_ref[0, pick, :] = jnp.where(at_encoder, key_grad, query_grad)
        stay_ref[1, pick, :] = jnp.where(at_encoder, value_grad, empty)
        send_ref[0, pick, :] = jnp.where(at_encoder, query_grad, key_grad)
        send_ref[1, pick, :] = jnp.where(at_encoder, empty, value_grad)


def attention(lengths, side, keep, recv, segment):
    shape = jax.ShapeDtypeStruct(keep.shape, BF)
    whole = pl.BlockSpec(memory_space=pltpu.VMEM)
    scalars = pl.BlockSpec(memory_space=pltpu.SMEM)
    return pl.pallas_call(
        attention_kernel,
        out_shape=(shape, shape),
        in_specs=[scalars, scalars, whole, whole, whole],
        out_specs=(whole, whole),
        compiler_params=pltpu.CompilerParams(vmem_limit_bytes=32 * 1024 * 1024),
    )(lengths, side, keep, recv, segment)


def gather_weights(weights, own_y, own_z, own_c):
    rows, parts, columns = weights.shape
    x_size, y_size, z_size = (lax.axis_size(a) for a in ("x", "y", "z"))
    slices = weights.reshape(rows, parts, x_size, columns // x_size).transpose(2, 1, 0, 3)
    chunk = lax.all_to_all(slices, "x", 0, 0, tiled=True)
    chunk = chunk.transpose(1, 0, 2, 3)
    full = jnp.zeros((parts, y_size, x_size, z_size, rows, columns // x_size), BF)

    def put(full, piece, part, from_y, from_z):
        half = jnp.where(from_y == own_c, 0, 1)
        return lax.dynamic_update_slice(
            full, piece[:, None, :, None], (part, half, 0, from_z % z_size, 0, 0)
        )

    def place(full, piece, part, from_z):
        full = put(full, piece, part, own_y, from_z)
        return put(full, shift(piece, "y", 1), part, 1 - own_y, from_z)

    full = place(full, chunk, 0, own_z)
    up = down = chunk
    for step in range(1, z_size // 2):
        up = shift(up, "z", 1)
        down = shift(down, "z", -1)
        full = place(full, up, 0, own_z - step)
        full = place(full, down, 0, own_z + step)
    up = shift(up[:1], "z", 1)
    down = shift(down[1:], "z", -1)
    full = place(full, up, 0, own_z + z_size // 2)
    full = place(full, down, 1, own_z + z_size // 2)
    return full.reshape(parts, y_size, x_size * z_size * rows, columns // x_size)


def decoder_shift(block, axis, distance):
    size = lax.axis_size(axis)
    route = [(size + i, size + (i + distance) % size) for i in range(size)]
    return lax.ppermute(block, ("section", axis), route)


def on_device(section_rows, norm_gains, proj_weights, section_cotan, enc_lengths, dec_segments):
    side = lax.axis_index("section")
    own_x, own_y, own_z, own_c = (lax.axis_index(a) for a in ("x", "y", "z", "mp"))
    x_size = lax.axis_size("x")
    at_encoder = side == 0
    rows, cotan, weights = section_rows[0], section_cotan[0], proj_weights[0]
    row_count, half_width = rows.shape
    width = 2 * half_width
    gain = norm_gains[0].astype(F32)
    wide_rows = rows.astype(F32)

    full = gather_weights(weights, own_y, own_z, own_c)

    square = jnp.sum(wide_rows * wide_rows, -1, keepdims=True)
    inverse = lax.rsqrt((square + shift(square, "mp", 1)) / width + EPS)
    normed = (wide_rows * inverse * gain).astype(BF)
    first_left = jnp.concatenate([normed] + [shift(normed, "x", -r) for r in range(1, x_size)], 0)
    far_cotan = [decoder_shift(cotan, "x", -r) for r in range(1, x_size)]
    cotan_rows = jnp.concatenate([cotan] + far_cotan, 0)
    second_left = jnp.where(at_encoder, first_left, cotan_rows)
    first_other = shift(first_left, "mp", 1)
    second_other = jnp.where(at_encoder, first_other, decoder_shift(cotan_rows, "mp", 1))

    small = jnp.concatenate([dec_segments[0], enc_lengths[0]])
    small = lax.all_gather(small, "x")
    small = jnp.concatenate([small, small], 0)
    small = lax.dynamic_slice_in_dim(small, own_x, x_size, 0)
    segment, lengths = small[:, :row_count], small[:, row_count:]

    def project(left, other, part):
        return (
            dot(left, full[part, 0], ((1,), (0,))) + dot(other, full[part, 1], ((1,), (0,)))
        ).astype(BF)

    packed = jnp.stack(
        (project(first_left, first_other, 0), project(second_left, second_other, 1)), 0
    )
    half = packed.shape[2] // 2
    keep = lax.dynamic_slice_in_dim(packed, side * half, half, 2)
    send = lax.dynamic_slice_in_dim(packed, (1 - side) * half, half, 2)
    recv = shift(send, "section", 1)
    stay, back = attention(lengths, side[None], keep, recv, segment[:, :, None])
    back = shift(back, "section", 1)
    grads = jnp.concatenate(
        (jnp.where(at_encoder, stay, back), jnp.where(at_encoder, back, stay)), 2
    )
    other_grads = shift(grads, "mp", 1)
    other_full = shift(full[:, 1], "mp", 1)

    def upstream_part(block):
        pick = slice(block * row_count, (block + 1) * row_count)
        total = 0.0
        for part in range(2):
            total += dot(grads[part, pick], full[part, 0], ((1,), (1,)))
            total += dot(other_grads[part, pick], other_full[part], ((1,), (1,)))
        return total

    upstream = upstream_part(0)
    for block in (2, 1, 3):
        upstream += shift(upstream_part(block).astype(BF), "x", block).astype(F32)

    wide_cotan = cotan.astype(F32)
    upstream += jnp.where(at_encoder, wide_cotan, 0.0)
    gain_grad = gain * upstream
    row_dot = jnp.sum(wide_rows * gain_grad, -1, keepdims=True)
    row_dot = (row_dot + shift(row_dot, "mp", 1)) / width
    result = inverse * gain_grad - wide_rows * inverse**3 * row_dot
    return (result + jnp.where(at_encoder, 0.0, wide_cotan))[None]


def solution(mesh):
    names = ("section", "y", "x", "z", "mp")
    split = Mesh(mesh.devices.reshape(2, 2, 4, 8, 2), names)
    fsdp = ("y", "x", "z")
    return jax.shard_map(
        on_device,
        mesh=split,
        in_specs=(
            P("section", fsdp, "mp"),
            P("section", "mp"),
            P("section", fsdp, None, "mp"),
            P("section", fsdp, "mp"),
            P(fsdp, None),
            P(fsdp, None),
        ),
        out_specs=P("section", fsdp, "mp"),
        check_vma=False,
    )
```

```python
import functools

import jax
import jax.numpy as jnp
import numpy as np
from jax import lax
from jax.experimental import pallas as pl
from jax.experimental.pallas import tpu as pltpu
from jax.sharding import Mesh, PartitionSpec as P

HD = 64
ELEN = 64
EPS = 1e-06
BF = jnp.bfloat16
F32 = jnp.float32
MIB = 1024 * 1024
META = 16
PIECES = 9


def shift(block, axis, distance):
    size = lax.axis_size(axis)
    return lax.ppermute(block, axis, [(i, (i + distance) % size) for i in range(size)])


def dot(left, right, contract):
    return lax.dot_general(left, right, (contract, ((), ())), preferred_element_type=F32)


def attention_kernel(place_ref, meta_ref, *refs):
    keep_refs, recv_refs, (stay_ref, send_ref) = refs[:2], refs[2:4], refs[4:]
    at_encoder = place_ref[0] == 0
    rows = 2 * ELEN
    query_index = lax.broadcasted_iota(jnp.int32, (rows, rows), 0).astype(F32)
    key_place = lax.broadcasted_iota(jnp.int32, (rows, rows), 1)
    key_slot = (key_place >= ELEN).astype(F32)
    key_index = key_place.astype(F32)
    lane = lax.broadcasted_iota(jnp.int32, (rows, 2 * HD), 1)
    for block in range(meta_ref.shape[0]):
        pick = pl.ds(block * rows, rows)
        kept = [ref[pick, :] for ref in keep_refs]
        received = [ref[pick, :] for ref in recv_refs]
        query, output_grad = [jnp.where(at_encoder, r, k) for k, r in zip(kept, received)]
        keys, values = [jnp.where(at_encoder, k, r) for k, r in zip(kept, received)]
        meta = meta_ref[block].astype(F32)
        own_slot = (query_index >= meta[:1, 0:1]).astype(F32)
        key_end = jnp.where(key_slot > 0, meta[:1, 2:3] + ELEN, meta[:1, 1:2])
        allowed = (own_slot == key_slot) & (key_index < key_end)
        sums = None
        for head in range(2):
            mine = lane // HD == head
            query_head = jnp.where(mine, query, 0)
            grad_head = jnp.where(mine, output_grad, 0)
            scores = dot(query_head, keys, ((1,), (1,)))
            scores = jnp.where(allowed, scores, -1e30)
            exponent = jnp.exp(scores - jnp.max(scores, -1, keepdims=True))
            softmax_rows = exponent / jnp.sum(exponent, -1, keepdims=True)
            soft_low = softmax_rows.astype(BF)
            attended = dot(soft_low, values, ((1,), (0,))).astype(BF)
            row_delta = jnp.sum(grad_head.astype(F32) * attended.astype(F32), -1, keepdims=True)
            prob_grad = dot(grad_head, values, ((1,), (1,)))
            score_grad = (softmax_rows * (prob_grad - row_delta)).astype(BF)
            query_grad = dot(score_grad, keys, ((1,), (0,)))
            key_grad = dot(score_grad, query, ((0,), (0,)))
            value_grad = dot(soft_low, output_grad, ((0,), (0,)))
            grads = (query_grad, key_grad, value_grad)
            sums = grads if head == 0 else [jnp.where(mine, g, s) for g, s in zip(grads, sums)]
        query_grad, key_grad, value_grad = [g.astype(BF) for g in sums]
        empty = jnp.zeros_like(query_grad)
        stay_ref[0, pick, :] = jnp.where(at_encoder, key_grad, query_grad)
        stay_ref[1, pick, :] = jnp.where(at_encoder, value_grad, empty)
        send_ref[0, pick, :] = jnp.where(at_encoder, query_grad, key_grad)
        send_ref[1, pick, :] = jnp.where(at_encoder, empty, value_grad)


def attention(place, meta, keep, recv):
    shape = jax.ShapeDtypeStruct((2,) + keep[0].shape, BF)
    whole = pl.BlockSpec(memory_space=pltpu.VMEM)
    return pl.pallas_call(
        attention_kernel,
        out_shape=(shape, shape),
        in_specs=[pl.BlockSpec(memory_space=pltpu.SMEM)] + [whole] * 5,
        out_specs=(whole, whole),
        compiler_params=pltpu.CompilerParams(vmem_limit_bytes=8 * MIB),
    )(place, meta, *keep, *recv)


def swap_halves(even, odd, lane):
    low = lane < HD
    return (
        jnp.where(low, even, pltpu.roll(odd, HD, 1)),
        jnp.where(low, pltpu.roll(even, HD, 1), odd),
    )


def prepare_kernel(
    place_ref,
    lengths_ref,
    segments_ref,
    rows_ref,
    cotan_ref,
    gain_ref,
    square_ref,
    earlier_ref,
    inverse_ref,
    out_ref,
):
    at_encoder = place_ref[0] == 0
    row_count, half_width = rows_ref.shape
    inverse = lax.rsqrt(square_ref[...] / (2 * half_width) + EPS)
    inverse_ref[...] = inverse
    first_count = row_count - jnp.sum(segments_ref[...].astype(F32), -1, keepdims=True)
    at = lax.broadcasted_iota(jnp.int32, (META, half_width), 1)
    lengths = [lengths_ref[0, slot].astype(F32) for slot in range(2)]
    meta = jnp.where(at == 1, lengths[0], jnp.where(at == 2, lengths[1], 0.0))
    out_ref[pl.ds(2 * row_count, META), :] = jnp.where(at == 0, first_count, meta).astype(BF)
    tile = 2 * HD
    lane = lax.broadcasted_iota(jnp.int32, (row_count, tile), 1)
    step = half_width // 4
    for j in range(step // tile):
        for couple in range(2):
            normed, second = [], []
            for x in (2 * couple, 2 * couple + 1):
                pick = pl.ds(x * step + j * tile, tile)
                wide = rows_ref[:, pick].astype(F32) * inverse * gain_ref[:, pick].astype(F32)
                normed.append(wide)
                second.append(jnp.where(at_encoder, wide, cotan_ref[:, pick].astype(F32)))
            for part, pair in enumerate((normed, second)):
                for odd, moved in enumerate(swap_halves(*pair, lane)):
                    start = (2 * j + odd) * 4 * HD + couple * tile
                    out_ref[pl.ds(part * row_count, row_count), pl.ds(start, tile)] = moved.astype(BF)


def prepare(place, lengths, segments, rows, cotan, gain, square, earlier):
    whole = pl.BlockSpec(memory_space=pltpu.VMEM)
    scalars = pl.BlockSpec(memory_space=pltpu.SMEM)
    return pl.pallas_call(
        prepare_kernel,
        out_shape=(
            jax.ShapeDtypeStruct(square.shape, F32),
            jax.ShapeDtypeStruct((2 * rows.shape[0] + META, rows.shape[1]), BF),
        ),
        in_specs=[scalars, scalars] + [whole] * 5 + [pl.BlockSpec(memory_space=pl.ANY)],
        out_specs=(whole, whole),
        compiler_params=pltpu.CompilerParams(vmem_limit_bytes=5 * MIB),
    )(place, lengths, segments, rows, cotan, gain, square, earlier)


def join(refs, pick):
    return jnp.concatenate([ref[:, pick].astype(F32) for ref in refs], 0)


def finish_kernel(place_ref, rows_ref, cotan_ref, gain_ref, *refs):
    parts, (grad_ref, dot_ref) = refs[:-2], refs[-2:]
    keep_cotan = jnp.where(place_ref[0] == 0, 1.0, 0.0)
    row_count, half_width = rows_ref.shape
    tile = 2 * HD
    lane = lax.broadcasted_iota(jnp.int32, (row_count, tile), 1)
    step = half_width // 4
    total = jnp.zeros((row_count, tile), F32)
    for j in range(step // tile):
        for couple in range(2):
            pair = []
            for odd in range(2):
                pick = pl.ds((2 * j + odd) * 4 * HD + couple * tile, tile)
                pair.append(parts[0][:, pick] + join(parts[1:3], pick) + join(parts[3:5], pick))
            for odd, upstream in enumerate(swap_halves(*pair, lane)):
                pick = pl.ds((2 * couple + odd) * step + j * tile, tile)
                upstream = upstream + keep_cotan * cotan_ref[:, pick].astype(F32)
                gain_grad = gain_ref[:, pick].astype(F32) * upstream
                grad_ref[:, pick] = gain_grad
                total = total + rows_ref[:, pick].astype(F32) * gain_grad
    dot_ref[...] = jnp.sum(total, -1, keepdims=True)


def finish(place, rows, cotan, gain, parts):
    whole = pl.BlockSpec(memory_space=pltpu.VMEM)
    return pl.pallas_call(
        finish_kernel,
        out_shape=(
            jax.ShapeDtypeStruct(rows.shape, F32),
            jax.ShapeDtypeStruct((rows.shape[0], 1), F32),
        ),
        in_specs=[pl.BlockSpec(memory_space=pltpu.SMEM)] + [whole] * (3 + len(parts)),
        out_specs=(whole, whole),
        compiler_params=pltpu.CompilerParams(vmem_limit_bytes=8 * MIB),
    )(place, rows, cotan, gain, *parts)


def weight_copies(own_z, piece_refs, weight_ref, sems):
    z_size = weight_ref.shape[1]
    distances = [0]
    for step in range(1, z_size // 2):
        distances += [-step, step]
    pairs = [
        (ref, weight_ref.at[:, lax.rem(own_z + distance + z_size, z_size)])
        for ref, distance in zip(piece_refs, distances)
    ]
    far = lax.rem(own_z + z_size // 2, z_size)
    half = piece_refs[-1].shape[1]
    for at in range(2):
        pairs.append((piece_refs[at - 2], weight_ref.at[:, far, pl.ds(at * half, half)]))
    return [
        pltpu.make_async_copy(source, there, sems.at[at]) for at, (source, there) in enumerate(pairs)
    ]


def project_kernel(part, place_ref, gathered_ref, *refs):
    piece_refs = refs[:PIECES]
    own_ref, other_ref, meta_ref, weight_ref, left_ref, left_sems, sems = refs[PIECES:]
    blocks = gathered_ref.shape[0]
    rows = left_ref.shape[0] // blocks
    copies = []
    for at in range(blocks):
        source = gathered_ref.at[lax.rem(place_ref[2] + at, blocks)]
        there = left_ref.at[pl.ds(at * rows, rows)]
        copies.append((source.at[pl.ds(part * rows, rows)], there, left_sems.at[0, at]))
        meta = source.at[pl.ds(2 * rows, META), pl.ds(0, 2 * HD)]
        copies.append((meta, meta_ref.at[at], left_sems.at[1, at]))
    copies = [pltpu.make_async_copy(*copy) for copy in copies]
    copies += weight_copies(place_ref[1], piece_refs, weight_ref, sems)
    for copy in copies:
        copy.start()
    for copy in copies:
        copy.wait()
    half = own_ref.shape[2]
    z_size, depth, width = weight_ref.shape[1:]
    for columns, out_ref in enumerate((own_ref, other_ref)):
        weights = weight_ref[columns].reshape(z_size * depth, width)
        product = dot(left_ref[...], weights, ((1,), (0,)))
        for at in range(2):
            out_ref[at] = product[:, at * half : (at + 1) * half].astype(out_ref.dtype)


def project(part, place, gathered, pieces):
    blocks, rows, width = gathered.shape
    rows = (rows - META) // 2
    _, depth, columns = pieces[0].shape
    shape = (2, blocks * rows, columns // 2)
    whole = pl.BlockSpec(memory_space=pltpu.VMEM)
    return pl.pallas_call(
        functools.partial(project_kernel, part),
        out_shape=(
            jax.ShapeDtypeStruct(shape, F32),
            jax.ShapeDtypeStruct(shape, BF),
            jax.ShapeDtypeStruct((blocks, META, 2 * HD), BF),
            jax.ShapeDtypeStruct((2, width // depth, depth, columns), BF),
        ),
        in_specs=[pl.BlockSpec(memory_space=pltpu.SMEM)]
        + [pl.BlockSpec(memory_space=pltpu.HBM)] * (1 + len(pieces)),
        out_specs=(whole, whole, whole, whole),
        scratch_shapes=[
            pltpu.VMEM((blocks * rows, width), BF),
            pltpu.SemaphoreType.DMA((2, blocks)),
            pltpu.SemaphoreType.DMA((PIECES,)),
        ],
        compiler_params=pltpu.CompilerParams(vmem_limit_bytes=56 * MIB),
    )(place, gathered, *pieces)


def back_kernel(place_ref, *refs):
    grad_refs, weight_refs = refs[:4], refs[4:6]
    own_ref, near_ref, far_ref, last_ref = refs[6:]
    at_encoder = place_ref[0] == 0
    rows = own_ref.shape[0]
    grads = []
    for part in range(2):
        for columns in range(2):
            stay, back = grad_refs[2 * columns][part], grad_refs[2 * columns + 1][part]
            low = jnp.where(at_encoder, stay, back)
            high = jnp.where(at_encoder, back, stay)
            grads.append((part, columns, jnp.concatenate([low, high], 1)))
    z_size, depth = weight_refs[0].shape[1:3]
    for z in range(z_size):
        total = 0.0
        for part, columns, grad in grads:
            total += dot(grad, weight_refs[part][columns, z], ((1,), (1,)))
        pick = pl.ds(z * depth, depth)
        for at, ref in enumerate((own_ref, near_ref, far_ref, last_ref)):
            ref[:, pick] = total[at * rows : (at + 1) * rows].astype(ref.dtype)


def back_project(place, grads, weights, shape):
    whole = pl.BlockSpec(memory_space=pltpu.VMEM)
    return pl.pallas_call(
        back_kernel,
        out_shape=[jax.ShapeDtypeStruct(shape, kind) for kind in (F32, F32, BF, F32)],
        in_specs=[pl.BlockSpec(memory_space=pltpu.SMEM)] + [whole] * (len(grads) + len(weights)),
        out_specs=[whole] * 4,
        compiler_params=pltpu.CompilerParams(vmem_limit_bytes=16 * MIB),
    )(place, *grads, *weights)


def exchange_columns(weights):
    rows, parts, columns = weights.shape
    x_size = lax.axis_size("x")
    slices = weights.reshape(rows, parts, x_size, columns // x_size).transpose(2, 1, 0, 3)
    return lax.all_to_all(slices, "x", 0, 0, tiled=True)


def gather_weights(chunk, own_y, own_c):
    x_size, rows, columns = chunk.shape
    z_size = lax.axis_size("z")
    at_source = own_y == own_c
    near = lax.ppermute(chunk, ("y", "mp"), [(1, 0), (2, 3), (0, 2), (3, 1)])
    far = lax.ppermute(chunk, ("y", "mp"), [(1, 2), (2, 1)])
    merged = jnp.stack([jnp.where(at_source, chunk, near), jnp.where(at_source, near, far)], 0)
    up = down = merged.reshape(2, x_size * rows, columns)
    pieces = [up]
    for step in range(1, z_size // 2):
        up, down = shift(up, "z", 1), shift(down, "z", -1)
        pieces += [up, down]
    half = x_size * rows // 2
    return pieces + [shift(up[:, :half], "z", 1), shift(down[:, half:], "z", -1)]


def sum_over_x(own, near, far, last):
    half = own.shape[0] // 2
    up, down = shift(far[:half], "x", 1), shift(far[half:], "x", -1)
    below_rest = shift(near[half:].astype(BF), "x", 1)
    above_rest = shift(last[:half].astype(BF), "x", -1)
    below = shift((near[:half] + up.astype(F32)).astype(BF), "x", 1)
    above = shift((last[half:] + down.astype(F32)).astype(BF), "x", -1)
    return own, below, below_rest, above_rest, above


def on_device(section_rows, norm_gains, proj_weights, section_cotan, enc_lengths, dec_segments):
    side = lax.axis_index("section")
    own_y, own_z, own_c = (lax.axis_index(a) for a in ("y", "z", "mp"))
    at_encoder = side == 0
    rows, cotan, weights = section_rows[0], section_cotan[0], proj_weights[0]
    row_count, half_width = rows.shape
    width = 2 * half_width
    place = jnp.stack([side, own_z, lax.axis_index("x")])
    wide_rows = rows.astype(F32)

    square = jnp.sum(wide_rows * wide_rows, -1, keepdims=True)
    square = square + shift(square, "mp", 1)
    chunks = exchange_columns(weights)
    inverse, left = prepare(
        place, enc_lengths, dec_segments, rows, cotan, norm_gains, square, chunks
    )
    gathered = lax.all_gather(left, "x")
    pieces = [gather_weights(chunks[:, part], own_y, own_c) for part in range(2)]

    keep, recv, full = [], [], []
    for part in range(2):
        own, other, meta, assembled = project(part, place, gathered, pieces[part])
        full.append(assembled)
        other = shift(other, "mp", 1)

        def half(at):
            picked = [lax.dynamic_index_in_dim(whole, at, 0, False) for whole in (own, other)]
            return (picked[0] + picked[1].astype(F32)).astype(BF)

        recv.append(shift(half(1 - side), "section", 1))
        keep.append(half(side))
    stay, back = attention(place, meta, keep, recv)
    back = shift(back, "section", 1)
    grads = (stay, back, shift(stay, "mp", 1), shift(back, "mp", 1))
    parts = sum_over_x(*back_project(place, grads, full, rows.shape))
    gain_grad, row_dot = finish(place, rows, cotan, norm_gains, parts)
    row_dot = (row_dot + shift(row_dot, "mp", 1)) / width
    result = inverse * gain_grad - wide_rows * inverse**3 * row_dot
    return (result + jnp.where(at_encoder, 0.0, cotan.astype(F32)))[None]


def solution(mesh):
    names = ("section", "y", "x", "z", "mp")
    split = Mesh(mesh.devices.reshape(2, 2, 4, 8, 2), names)
    fsdp = ("y", "x", "z")
    return jax.shard_map(
        on_device,
        mesh=split,
        in_specs=(
            P("section", fsdp, "mp"),
            P("section", "mp"),
            P("section", fsdp, None, "mp"),
            P("section", fsdp, "mp"),
            P(fsdp, None),
            P(fsdp, None),
        ),
        out_specs=P("section", fsdp, "mp"),
        check_vma=False,
    )
```

```python
import functools

import jax
import jax.numpy as jnp
import numpy as np
from jax import lax
from jax.experimental import pallas as pl
from jax.experimental.pallas import tpu as pltpu
from jax.sharding import Mesh, PartitionSpec as P

HD = 64
ELEN = 64
EPS = 1e-06
BF = jnp.bfloat16
F32 = jnp.float32
MIB = 1024 * 1024
META = 16
PIECES = 9
BLOCKS = 4
PROJECT_LIMIT = 56


def shift(block, axis, distance):
    size = lax.axis_size(axis)
    return lax.ppermute(block, axis, [(i, (i + distance) % size) for i in range(size)])


def dot(left, right, contract):
    return lax.dot_general(left, right, (contract, ((), ())), preferred_element_type=F32)


def side_by_side(heads):
    half = heads.shape[0] // 2
    return jnp.concatenate([heads[:half], heads[half:]], 1)


def attention_kernel(place_ref, meta_ref, *refs):
    keep_refs, recv_refs, (stay_ref, send_ref) = refs[:2], refs[2:4], refs[4:]
    at_encoder = place_ref[0] == 0
    rows = 2 * ELEN
    query_index = lax.broadcasted_iota(jnp.int32, (rows, rows), 0).astype(F32)
    key_place = lax.broadcasted_iota(jnp.int32, (rows, rows), 1)
    key_slot = (key_place >= ELEN).astype(F32)
    key_index = key_place.astype(F32)
    lane = lax.broadcasted_iota(jnp.int32, (rows, 2 * HD), 1)
    for block in range(meta_ref.shape[0]):
        pick = pl.ds(block * rows, rows)
        kept = [ref[pick, :] for ref in keep_refs]
        received = [ref[pick, :] for ref in recv_refs]
        query, output_grad = [jnp.where(at_encoder, r, k) for k, r in zip(kept, received)]
        keys, values = [jnp.where(at_encoder, k, r) for k, r in zip(kept, received)]
        meta = meta_ref[block].astype(F32)
        own_slot = (query_index >= meta[:1, 0:1]).astype(F32)
        key_end = jnp.where(key_slot > 0, meta[:1, 2:3] + ELEN, meta[:1, 1:2])
        allowed = (own_slot == key_slot) & (key_index < key_end)
        allowed = jnp.concatenate([allowed.astype(F32)] * 2, 0) > 0
        query, output_grad, key_heads, value_heads = [
            jnp.concatenate([jnp.where(lane // HD == head, part, 0) for head in range(2)], 0)
            for part in (query, output_grad, keys, values)
        ]
        scores = dot(query, keys, ((1,), (1,)))
        prob_grad = dot(output_grad, values, ((1,), (1,)))
        scores = jnp.where(allowed, scores, -1e30)
        exponent = jnp.exp(scores - jnp.max(scores, -1, keepdims=True))
        softmax_rows = exponent / jnp.sum(exponent, -1, keepdims=True)
        soft_low = softmax_rows.astype(BF)
        attended = dot(side_by_side(soft_low), value_heads, ((1,), (0,))).astype(BF).astype(F32)
        attended = jnp.concatenate([attended, attended], 0)
        row_delta = jnp.sum(output_grad.astype(F32) * attended, -1, keepdims=True)
        score_grad = (softmax_rows * (prob_grad - row_delta)).astype(BF)
        query_grad = dot(side_by_side(score_grad), key_heads, ((1,), (0,))).astype(BF)
        key_grad = dot(score_grad, query, ((0,), (0,))).astype(BF)
        value_grad = dot(soft_low, output_grad, ((0,), (0,))).astype(BF)
        empty = jnp.zeros_like(query_grad)
        stay_ref[0, pick, :] = jnp.where(at_encoder, key_grad, query_grad)
        stay_ref[1, pick, :] = jnp.where(at_encoder, value_grad, empty)
        send_ref[0, pick, :] = jnp.where(at_encoder, query_grad, key_grad)
        send_ref[1, pick, :] = jnp.where(at_encoder, empty, value_grad)


def attention(place, meta, keep, recv):
    shape = jax.ShapeDtypeStruct((2,) + keep[0].shape, BF)
    whole = pl.BlockSpec(memory_space=pltpu.VMEM)
    return pl.pallas_call(
        attention_kernel,
        out_shape=(shape, shape),
        in_specs=[pl.BlockSpec(memory_space=pltpu.SMEM)] + [whole] * 5,
        out_specs=(whole, whole),
        compiler_params=pltpu.CompilerParams(vmem_limit_bytes=8 * MIB),
    )(place, meta, *keep, *recv)


def swap_halves(even, odd, lane):
    low = lane < HD
    return (
        jnp.where(low, even, pltpu.roll(odd, HD, 1)),
        jnp.where(low, pltpu.roll(even, HD, 1), odd),
    )


def prepare_kernel(
    place_ref,
    lengths_ref,
    segments_ref,
    rows_ref,
    cotan_ref,
    gain_ref,
    square_ref,
    earlier_ref,
    inverse_ref,
    out_ref,
):
    at_encoder = place_ref[0] == 0
    row_count, half_width = rows_ref.shape
    inverse = lax.rsqrt(square_ref[...] / (2 * half_width) + EPS)
    inverse_ref[...] = inverse
    first_count = row_count - jnp.sum(segments_ref[...].astype(F32), -1, keepdims=True)
    at = lax.broadcasted_iota(jnp.int32, (META, half_width), 1)
    lengths = [lengths_ref[0, slot].astype(F32) for slot in range(2)]
    meta = jnp.where(at == 1, lengths[0], jnp.where(at == 2, lengths[1], 0.0))
    out_ref[pl.ds(2 * row_count, META), :] = jnp.where(at == 0, first_count, meta).astype(BF)
    tile = 2 * HD
    lane = lax.broadcasted_iota(jnp.int32, (row_count, tile), 1)
    step = half_width // 4
    for j in range(step // tile):
        for couple in range(2):
            normed, second = [], []
            for x in (2 * couple, 2 * couple + 1):
                pick = pl.ds(x * step + j * tile, tile)
                wide = rows_ref[:, pick].astype(F32) * inverse * gain_ref[:, pick].astype(F32)
                normed.append(wide)
                second.append(jnp.where(at_encoder, wide, cotan_ref[:, pick].astype(F32)))
            for part, pair in enumerate((normed, second)):
                for odd, moved in enumerate(swap_halves(*pair, lane)):
                    start = (2 * j + odd) * 4 * HD + couple * tile
                    out_ref[pl.ds(part * row_count, row_count), pl.ds(start, tile)] = moved.astype(BF)


def prepare(place, lengths, segments, rows, cotan, gain, square, earlier):
    whole = pl.BlockSpec(memory_space=pltpu.VMEM)
    scalars = pl.BlockSpec(memory_space=pltpu.SMEM)
    return pl.pallas_call(
        prepare_kernel,
        out_shape=(
            jax.ShapeDtypeStruct(square.shape, F32),
            jax.ShapeDtypeStruct((2 * rows.shape[0] + META, rows.shape[1]), BF),
        ),
        in_specs=[scalars, scalars] + [whole] * 5 + [pl.BlockSpec(memory_space=pl.ANY)],
        out_specs=(whole, whole),
        compiler_params=pltpu.CompilerParams(vmem_limit_bytes=5 * MIB),
    )(place, lengths, segments, rows, cotan, gain, square, earlier)


def join(refs, pick):
    return jnp.concatenate([ref[:, pick].astype(F32) for ref in refs], 0)


def finish_kernel(place_ref, rows_ref, cotan_ref, gain_ref, *refs):
    parts, (grad_ref, dot_ref) = refs[:-2], refs[-2:]
    keep_cotan = jnp.where(place_ref[0] == 0, 1.0, 0.0)
    row_count, half_width = rows_ref.shape
    tile = 2 * HD
    lane = lax.broadcasted_iota(jnp.int32, (row_count, tile), 1)
    step = half_width // 4
    total = jnp.zeros((row_count, tile), F32)
    for j in range(step // tile):
        for couple in range(2):
            pair = []
            for odd in range(2):
                pick = pl.ds((2 * j + odd) * 4 * HD + couple * tile, tile)
                pair.append(parts[0][:, pick] + join(parts[1:3], pick) + join(parts[3:5], pick))
            for odd, upstream in enumerate(swap_halves(*pair, lane)):
                pick = pl.ds((2 * couple + odd) * step + j * tile, tile)
                upstream = upstream + keep_cotan * cotan_ref[:, pick].astype(F32)
                gain_grad = gain_ref[:, pick].astype(F32) * upstream
                grad_ref[:, pick] = gain_grad
                total = total + rows_ref[:, pick].astype(F32) * gain_grad
    dot_ref[...] = jnp.sum(total, -1, keepdims=True)


def finish(place, rows, cotan, gain, parts):
    whole = pl.BlockSpec(memory_space=pltpu.VMEM)
    return pl.pallas_call(
        finish_kernel,
        out_shape=(
            jax.ShapeDtypeStruct(rows.shape, F32),
            jax.ShapeDtypeStruct((rows.shape[0], 1), F32),
        ),
        in_specs=[pl.BlockSpec(memory_space=pltpu.SMEM)] + [whole] * (3 + len(parts)),
        out_specs=(whole, whole),
        compiler_params=pltpu.CompilerParams(vmem_limit_bytes=30 * MIB),
    )(place, rows, cotan, gain, *parts)


def weight_copies(own_z, piece_refs, weight_ref, sems):
    z_size = weight_ref.shape[1]
    distances = [0]
    for step in range(1, z_size // 2):
        distances += [-step, step]
    pairs = [
        (ref, weight_ref.at[:, lax.rem(own_z + distance + z_size, z_size)])
        for ref, distance in zip(piece_refs, distances)
    ]
    far = lax.rem(own_z + z_size // 2, z_size)
    half = piece_refs[-1].shape[1]
    for at in range(2):
        pairs.append((piece_refs[at - 2], weight_ref.at[:, far, pl.ds(at * half, half)]))
    return [
        pltpu.make_async_copy(source, there, sems.at[at]) for at, (source, there) in enumerate(pairs)
    ]


def project_kernel(part, place_ref, gathered_ref, *refs):
    piece_refs = refs[:PIECES]
    own_ref, other_ref, meta_ref, out_ref, left_ref, weight_ref, left_sems, sems = refs[PIECES:]
    blocks = gathered_ref.shape[0]
    rows = left_ref.shape[0] // blocks
    copies = []
    for at in range(blocks):
        source = gathered_ref.at[lax.rem(place_ref[2] + at, blocks)]
        there = left_ref.at[pl.ds(at * rows, rows)]
        copies.append((source.at[pl.ds(part * rows, rows)], there, left_sems.at[0, at]))
        meta = source.at[pl.ds(2 * rows, META), pl.ds(0, 2 * HD)]
        copies.append((meta, meta_ref.at[at], left_sems.at[1, at]))
    copies = [pltpu.make_async_copy(*copy) for copy in copies]
    copies += weight_copies(place_ref[1], piece_refs, weight_ref, sems)
    for copy in copies:
        copy.start()
    for copy in copies:
        copy.wait()
    assembled = pltpu.make_async_copy(weight_ref, out_ref, left_sems.at[2, 0])
    assembled.start()
    half = own_ref.shape[2]
    z_size, depth, width = weight_ref.shape[1:]
    for columns, ref in ((1, other_ref), (0, own_ref)):
        weights = weight_ref[columns].reshape(z_size * depth, width)
        product = dot(left_ref[...], weights, ((1,), (0,)))
        for at in range(2):
            ref[at] = product[:, at * half : (at + 1) * half].astype(ref.dtype)
    assembled.wait()


def project(part, place, gathered, pieces):
    blocks, rows, width = gathered.shape
    rows = (rows - META) // 2
    _, depth, columns = pieces[0].shape
    shape = (2, blocks * rows, columns // 2)
    weights = (2, width // depth, depth, columns)
    whole = pl.BlockSpec(memory_space=pltpu.VMEM)
    return pl.pallas_call(
        functools.partial(project_kernel, part),
        out_shape=(
            jax.ShapeDtypeStruct(shape, F32),
            jax.ShapeDtypeStruct(shape, BF),
            jax.ShapeDtypeStruct((blocks, META, 2 * HD), BF),
            jax.ShapeDtypeStruct(weights, BF),
        ),
        in_specs=[pl.BlockSpec(memory_space=pltpu.SMEM)]
        + [pl.BlockSpec(memory_space=pltpu.HBM)] * (1 + len(pieces)),
        out_specs=(whole, whole, whole, pl.BlockSpec(memory_space=pltpu.HBM)),
        scratch_shapes=[
            pltpu.VMEM((blocks * rows, width), BF),
            pltpu.VMEM(weights, BF),
            pltpu.SemaphoreType.DMA((3, blocks)),
            pltpu.SemaphoreType.DMA((PIECES,)),
        ],
        compiler_params=pltpu.CompilerParams(vmem_limit_bytes=PROJECT_LIMIT * MIB),
    )(place, gathered, *pieces)


def back_kernel(blocks, place_ref, *refs):
    grad_refs, weight_refs, out_refs = refs[:4], refs[4:6], refs[6:]
    at_encoder = place_ref[0] == 0
    rows = grad_refs[0].shape[1] // BLOCKS
    grads = []
    for part in range(2):
        for columns in range(2):
            picked = []
            for ref in grad_refs[2 * columns : 2 * columns + 2]:
                pieces = [ref[part, pl.ds(block * rows, rows)] for block in blocks]
                picked.append(jnp.concatenate(pieces, 0))
            low = jnp.where(at_encoder, picked[0], picked[1])
            high = jnp.where(at_encoder, picked[1], picked[0])
            grads.append((part, columns, jnp.concatenate([low, high], 1)))
    z_size, depth = weight_refs[0].shape[1:3]
    for z in range(z_size):
        total = 0.0
        for part, columns, grad in grads:
            total += dot(grad, weight_refs[part][columns, z], ((1,), (1,)))
        pick = pl.ds(z * depth, depth)
        start = 0
        for ref in out_refs:
            stop = start + ref.shape[0]
            ref[:, pick] = total[start:stop].astype(ref.dtype)
            start = stop


def back_project(blocks, outs, place, grads, weights):
    whole = pl.BlockSpec(memory_space=pltpu.VMEM)
    return pl.pallas_call(
        functools.partial(back_kernel, blocks),
        out_shape=outs,
        in_specs=[pl.BlockSpec(memory_space=pltpu.SMEM)] + [whole] * (len(grads) + len(weights)),
        out_specs=[whole] * len(outs),
        compiler_params=pltpu.CompilerParams(vmem_limit_bytes=16 * MIB),
    )(place, *grads, *weights)


def slice_columns(weights):
    rows, parts, columns = weights.shape
    x_size = lax.axis_size("x")
    return weights.reshape(rows, parts, x_size, columns // x_size).transpose(2, 1, 0, 3)


def gather_weights(chunk, at_source):
    x_size, rows, columns = chunk.shape
    z_size = lax.axis_size("z")
    near = lax.ppermute(chunk, ("y", "mp"), [(1, 0), (2, 3), (0, 2), (3, 1)])
    far = lax.ppermute(chunk, ("y", "mp"), [(1, 2), (2, 1)])
    merged = jnp.stack([jnp.where(at_source, chunk, near), jnp.where(at_source, near, far)], 0)
    up = down = merged.reshape(2, x_size * rows, columns)
    pieces = [up]
    for step in range(1, z_size // 2):
        up, down = shift(up, "z", 1), shift(down, "z", -1)
        pieces += [up, down]
    half = x_size * rows // 2
    return pieces + [shift(up[:, :half], "z", 1), shift(down[:, half:], "z", -1)]


def sum_over_x(far_low, far_high, own, near_low, near_high, last_low, last_high):
    up, down = shift(far_low, "x", 1), shift(far_high, "x", -1)
    below_high, above_low = shift(near_high, "x", 1), shift(last_low, "x", -1)
    below_low = shift((near_low + up.astype(F32)).astype(BF), "x", 1)
    above_high = shift((last_high + down.astype(F32)).astype(BF), "x", -1)
    return own, below_low, below_high, above_low, above_high


def on_device(section_rows, norm_gains, proj_weights, section_cotan, enc_lengths, dec_segments):
    side = lax.axis_index("section")
    own_y, own_z, own_c = (lax.axis_index(a) for a in ("y", "z", "mp"))
    rows, cotan, weights = section_rows[0], section_cotan[0], proj_weights[0]
    place = jnp.stack([side, own_z, lax.axis_index("x")])
    wide_rows = rows.astype(F32)

    square = jnp.sum(wide_rows * wide_rows, -1, keepdims=True)
    square = square + shift(square, "mp", 1)
    slices = slice_columns(weights)
    chunks = lax.all_to_all(slices, "x", 0, 0, tiled=True)
    inverse, left = prepare(
        place, enc_lengths, dec_segments, rows, cotan, norm_gains, square, chunks
    )
    gathered = lax.all_gather(left, "x")
    pieces = [gather_weights(chunks[:, part], own_y == own_c) for part in range(2)]

    keep, recv, full = [], [], []
    for part in range(2):
        own, other, meta, assembled = project(part, place, gathered, pieces[part])
        full.append(assembled)
        other = shift(other, "mp", 1)

        def half(at):
            picked = [lax.dynamic_index_in_dim(whole, at, 0, False) for whole in (own, other)]
            return (picked[0] + picked[1].astype(F32)).astype(BF)

        recv.append(shift(half(1 - side), "section", 1))
        keep.append(half(side))
    stay, back = attention(place, meta, keep, recv)
    back = shift(back, "section", 1)
    grads = (stay, back, shift(stay, "mp", 1), shift(back, "mp", 1))
    row_count, half_width = rows.shape

    def outs(*kinds):
        return [jax.ShapeDtypeStruct((row_count // 2, half_width), kind) for kind in kinds]

    far = back_project((2,), outs(BF, BF), place, grads, full)
    whole = [jax.ShapeDtypeStruct(rows.shape, F32)]
    near = back_project((0, 1, 3), whole + outs(F32, BF, BF, F32), place, grads, full)
    parts = sum_over_x(*far, *near)
    gain_grad, row_dot = finish(place, rows, cotan, norm_gains, parts)
    row_dot = (row_dot + shift(row_dot, "mp", 1)) / (2 * rows.shape[1])
    result = inverse * gain_grad - wide_rows * inverse**3 * row_dot
    return (result + jnp.where(side == 0, 0.0, cotan.astype(F32)))[None]


def solution(mesh):
    names = ("section", "y", "x", "z", "mp")
    split = Mesh(mesh.devices.reshape(2, 2, 4, 8, 2), names)
    fsdp = ("y", "x", "z")
    return jax.shard_map(
        on_device,
        mesh=split,
        in_specs=(
            P("section", fsdp, "mp"),
            P("section", "mp"),
            P("section", fsdp, None, "mp"),
            P("section", fsdp, "mp"),
            P(fsdp, None),
            P(fsdp, None),
        ),
        out_specs=P("section", fsdp, "mp"),
        check_vma=False,
    )
```

```python
import functools

import jax
import jax.numpy as jnp
import numpy as np
from jax import lax
from jax.experimental import pallas as pl
from jax.experimental.pallas import tpu as pltpu
from jax.sharding import Mesh, PartitionSpec as P

HD = 64
ELEN = 64
EPS = 1e-06
BF = jnp.bfloat16
F32 = jnp.float32
MIB = 1024 * 1024
META = 16
PIECES = 8
BLOCKS = 4
PROJECT_LIMIT = 56


def shift(block, axis, distance):
    size = lax.axis_size(axis)
    return lax.ppermute(block, axis, [(i, (i + distance) % size) for i in range(size)])


def dot(left, right, contract):
    return lax.dot_general(left, right, (contract, ((), ())), preferred_element_type=F32)


def side_by_side(heads):
    half = heads.shape[0] // 2
    return jnp.concatenate([heads[:half], heads[half:]], 1)


def attention_kernel(place_ref, meta_ref, *refs):
    keep_refs, recv_refs, (stay_ref, send_ref) = refs[:2], refs[2:4], refs[4:]
    at_encoder = place_ref[0] == 0
    rows = 2 * ELEN
    query_index = lax.broadcasted_iota(jnp.int32, (rows, rows), 0).astype(F32)
    key_place = lax.broadcasted_iota(jnp.int32, (rows, rows), 1)
    key_slot = (key_place >= ELEN).astype(F32)
    key_index = key_place.astype(F32)
    lane = lax.broadcasted_iota(jnp.int32, (rows, 2 * HD), 1)
    for block in range(meta_ref.shape[0]):
        pick = pl.ds(block * rows, rows)
        kept = [ref[pick, :] for ref in keep_refs]
        received = [ref[pick, :] for ref in recv_refs]
        query, output_grad = [jnp.where(at_encoder, r, k) for k, r in zip(kept, received)]
        keys, values = [jnp.where(at_encoder, k, r) for k, r in zip(kept, received)]
        meta = meta_ref[block].astype(F32)
        own_slot = (query_index >= meta[:1, 0:1]).astype(F32)
        key_end = jnp.where(key_slot > 0, meta[:1, 2:3] + ELEN, meta[:1, 1:2])
        allowed = (own_slot == key_slot) & (key_index < key_end)
        allowed = jnp.concatenate([allowed.astype(F32)] * 2, 0) > 0
        query, output_grad, key_heads, value_heads = [
            jnp.concatenate([jnp.where(lane // HD == head, part, 0) for head in range(2)], 0)
            for part in (query, output_grad, keys, values)
        ]
        scores = dot(query, keys, ((1,), (1,)))
        prob_grad = dot(output_grad, values, ((1,), (1,)))
        scores = jnp.where(allowed, scores, -1e30)
        exponent = jnp.exp(scores - jnp.max(scores, -1, keepdims=True))
        softmax_rows = exponent / jnp.sum(exponent, -1, keepdims=True)
        soft_low = softmax_rows.astype(BF)
        attended = dot(side_by_side(soft_low), value_heads, ((1,), (0,))).astype(BF).astype(F32)
        attended = jnp.concatenate([attended, attended], 0)
        row_delta = jnp.sum(output_grad.astype(F32) * attended, -1, keepdims=True)
        score_grad = (softmax_rows * (prob_grad - row_delta)).astype(BF)
        query_grad = dot(side_by_side(score_grad), key_heads, ((1,), (0,))).astype(BF)
        key_grad = dot(score_grad, query, ((0,), (0,))).astype(BF)
        value_grad = dot(soft_low, output_grad, ((0,), (0,))).astype(BF)
        empty = jnp.zeros_like(query_grad)
        stay_ref[0, pick, :] = jnp.where(at_encoder, key_grad, query_grad)
        stay_ref[1, pick, :] = jnp.where(at_encoder, value_grad, empty)
        send_ref[0, pick, :] = jnp.where(at_encoder, query_grad, key_grad)
        send_ref[1, pick, :] = jnp.where(at_encoder, empty, value_grad)


def attention(place, meta, keep, recv):
    shape = jax.ShapeDtypeStruct((2,) + keep[0].shape, BF)
    whole = pl.BlockSpec(memory_space=pltpu.VMEM)
    return pl.pallas_call(
        attention_kernel,
        out_shape=(shape, shape),
        in_specs=[pl.BlockSpec(memory_space=pltpu.SMEM)] + [whole] * 5,
        out_specs=(whole, whole),
        compiler_params=pltpu.CompilerParams(vmem_limit_bytes=8 * MIB),
    )(place, meta, *keep, *recv)


def swap_halves(even, odd, lane):
    low = lane < HD
    return (
        jnp.where(low, even, pltpu.roll(odd, HD, 1)),
        jnp.where(low, pltpu.roll(even, HD, 1), odd),
    )


def prepare_kernel(
    place_ref,
    lengths_ref,
    segments_ref,
    rows_ref,
    cotan_ref,
    gain_ref,
    square_ref,
    other_ref,
    earlier_ref,
    inverse_ref,
    out_ref,
):
    at_encoder = place_ref[0] == 0
    row_count, half_width = rows_ref.shape
    inverse = lax.rsqrt((square_ref[...] + other_ref[...]) / (2 * half_width) + EPS)
    inverse_ref[...] = inverse
    first_count = row_count - jnp.sum(segments_ref[...].astype(F32), -1, keepdims=True)
    at = lax.broadcasted_iota(jnp.int32, (META, half_width), 1)
    lengths = [lengths_ref[0, slot].astype(F32) for slot in range(2)]
    meta = jnp.where(at == 1, lengths[0], jnp.where(at == 2, lengths[1], 0.0))
    out_ref[pl.ds(2 * row_count, META), :] = jnp.where(at == 0, first_count, meta).astype(BF)
    tile = 2 * HD
    lane = lax.broadcasted_iota(jnp.int32, (row_count, tile), 1)
    step = half_width // 4
    for j in range(step // tile):
        for couple in range(2):
            normed, second = [], []
            for x in (2 * couple, 2 * couple + 1):
                pick = pl.ds(x * step + j * tile, tile)
                wide = rows_ref[:, pick].astype(F32) * inverse * gain_ref[:, pick].astype(F32)
                normed.append(wide)
                second.append(jnp.where(at_encoder, wide, cotan_ref[:, pick].astype(F32)))
            for part, pair in enumerate((normed, second)):
                for odd, moved in enumerate(swap_halves(*pair, lane)):
                    start = (2 * j + odd) * 4 * HD + couple * tile
                    out_ref[pl.ds(part * row_count, row_count), pl.ds(start, tile)] = moved.astype(BF)


def prepare(place, lengths, segments, rows, cotan, gain, square, other, earlier):
    whole = pl.BlockSpec(memory_space=pltpu.VMEM)
    scalars = pl.BlockSpec(memory_space=pltpu.SMEM)
    return pl.pallas_call(
        prepare_kernel,
        out_shape=(
            jax.ShapeDtypeStruct(square.shape, F32),
            jax.ShapeDtypeStruct((2 * rows.shape[0] + META, rows.shape[1]), BF),
        ),
        in_specs=[scalars, scalars] + [whole] * 6 + [pl.BlockSpec(memory_space=pl.ANY)],
        out_specs=(whole, whole),
        compiler_params=pltpu.CompilerParams(vmem_limit_bytes=5 * MIB),
    )(place, lengths, segments, rows, cotan, gain, square, other, earlier)


def join(refs, pick):
    return jnp.concatenate([ref[:, pick].astype(F32) for ref in refs], 0)


def finish_kernel(place_ref, rows_ref, cotan_ref, gain_ref, *refs):
    parts, (grad_ref, dot_ref) = refs[:-2], refs[-2:]
    keep_cotan = jnp.where(place_ref[0] == 0, 1.0, 0.0)
    row_count, half_width = rows_ref.shape
    tile = 2 * HD
    lane = lax.broadcasted_iota(jnp.int32, (row_count, tile), 1)
    step = half_width // 4
    total = jnp.zeros((row_count, tile), F32)
    for j in range(step // tile):
        for couple in range(2):
            pair = []
            for odd in range(2):
                pick = pl.ds((2 * j + odd) * 4 * HD + couple * tile, tile)
                pair.append(parts[0][:, pick] + join(parts[1:3], pick) + join(parts[3:5], pick))
            for odd, upstream in enumerate(swap_halves(*pair, lane)):
                pick = pl.ds((2 * couple + odd) * step + j * tile, tile)
                upstream = upstream + keep_cotan * cotan_ref[:, pick].astype(F32)
                gain_grad = gain_ref[:, pick].astype(F32) * upstream
                grad_ref[:, pick] = gain_grad
                total = total + rows_ref[:, pick].astype(F32) * gain_grad
    dot_ref[...] = jnp.sum(total, -1, keepdims=True)


def finish(place, rows, cotan, gain, parts):
    whole = pl.BlockSpec(memory_space=pltpu.VMEM)
    return pl.pallas_call(
        finish_kernel,
        out_shape=(
            jax.ShapeDtypeStruct(rows.shape, F32),
            jax.ShapeDtypeStruct((rows.shape[0], 1), F32),
        ),
        in_specs=[pl.BlockSpec(memory_space=pltpu.SMEM)] + [whole] * (3 + len(parts)),
        out_specs=(whole, whole),
        compiler_params=pltpu.CompilerParams(vmem_limit_bytes=30 * MIB),
    )(place, rows, cotan, gain, *parts)


def weight_copies(own_z, piece_refs, weight_ref, sems):
    z_size = weight_ref.shape[1]
    distances = [0]
    for step in range(1, z_size // 2):
        distances += [-step, step]
    distances.append(z_size // 2)
    pairs = [
        (ref, weight_ref.at[:, lax.rem(own_z + distance + z_size, z_size)])
        for ref, distance in zip(piece_refs, distances)
    ]
    return [
        pltpu.make_async_copy(source, there, sems.at[at]) for at, (source, there) in enumerate(pairs)
    ]


def project_kernel(part, place_ref, gathered_ref, *refs):
    piece_refs = refs[:PIECES]
    own_ref, other_ref, meta_ref, *out_refs = refs[PIECES : PIECES + 5]
    left_ref, weight_ref, left_sems, sems = refs[PIECES + 5 :]
    blocks = gathered_ref.shape[0]
    rows = left_ref.shape[0] // blocks
    copies = []
    for at in range(blocks):
        source = gathered_ref.at[lax.rem(place_ref[2] + at, blocks)]
        there = left_ref.at[pl.ds(at * rows, rows)]
        copies.append((source.at[pl.ds(part * rows, rows)], there, left_sems.at[0, at]))
        meta = source.at[pl.ds(2 * rows, META), pl.ds(0, 2 * HD)]
        copies.append((meta, meta_ref.at[at], left_sems.at[1, at]))
    copies = [pltpu.make_async_copy(*copy) for copy in copies]
    copies += weight_copies(place_ref[1], piece_refs, weight_ref, sems)
    for copy in copies:
        copy.start()
    for copy in copies:
        copy.wait()
    assembled = [
        pltpu.make_async_copy(weight_ref.at[at], ref, left_sems.at[2, at])
        for at, ref in enumerate(out_refs)
    ]
    for copy in assembled:
        copy.start()
    half = own_ref.shape[2]
    z_size, depth, width = weight_ref.shape[1:]
    for columns, ref in ((1, other_ref), (0, own_ref)):
        weights = weight_ref[columns].reshape(z_size * depth, width)
        product = dot(left_ref[...], weights, ((1,), (0,)))
        for at in range(2):
            ref[at] = product[:, at * half : (at + 1) * half].astype(ref.dtype)
    for copy in assembled:
        copy.wait()


def project(part, place, gathered, pieces):
    blocks, rows, width = gathered.shape
    rows = (rows - META) // 2
    _, depth, columns = pieces[0].shape
    shape = (2, blocks * rows, columns // 2)
    weights = (2, width // depth, depth, columns)
    whole = pl.BlockSpec(memory_space=pltpu.VMEM)
    return pl.pallas_call(
        functools.partial(project_kernel, part),
        out_shape=(
            jax.ShapeDtypeStruct(shape, F32),
            jax.ShapeDtypeStruct(shape, BF),
            jax.ShapeDtypeStruct((blocks, META, 2 * HD), BF),
        )
        + (jax.ShapeDtypeStruct(weights[1:], BF),) * 2,
        in_specs=[pl.BlockSpec(memory_space=pltpu.SMEM)]
        + [pl.BlockSpec(memory_space=pltpu.HBM)] * (1 + len(pieces)),
        out_specs=(whole,) * 3 + (pl.BlockSpec(memory_space=pltpu.HBM),) * 2,
        scratch_shapes=[
            pltpu.VMEM((blocks * rows, width), BF),
            pltpu.VMEM(weights, BF),
            pltpu.SemaphoreType.DMA((3, blocks)),
            pltpu.SemaphoreType.DMA((PIECES,)),
        ],
        compiler_params=pltpu.CompilerParams(vmem_limit_bytes=PROJECT_LIMIT * MIB),
    )(place, gathered, *pieces)


def back_kernel(blocks, place_ref, *refs):
    grad_refs, weight_refs, out_refs = refs[:4], refs[4:8], refs[8:]
    at_encoder = place_ref[0] == 0
    rows = grad_refs[0].shape[1] // BLOCKS
    grads = []
    for part in range(2):
        for columns in range(2):
            picked = []
            for ref in grad_refs[2 * columns : 2 * columns + 2]:
                pieces = [ref[part, pl.ds(block * rows, rows)] for block in blocks]
                picked.append(jnp.concatenate(pieces, 0))
            low = jnp.where(at_encoder, picked[0], picked[1])
            high = jnp.where(at_encoder, picked[1], picked[0])
            grads.append((part, columns, jnp.concatenate([low, high], 1)))
    z_size, depth = weight_refs[0].shape[:2]
    for z in range(z_size):
        total = 0.0
        for part, columns, grad in grads:
            total += dot(grad, weight_refs[2 * part + columns][z], ((1,), (1,)))
        pick = pl.ds(z * depth, depth)
        start = 0
        for ref in out_refs:
            stop = start + ref.shape[0]
            ref[:, pick] = total[start:stop].astype(ref.dtype)
            start = stop


def back_project(blocks, outs, place, grads, weights):
    whole = pl.BlockSpec(memory_space=pltpu.VMEM)
    return pl.pallas_call(
        functools.partial(back_kernel, blocks),
        out_shape=outs,
        in_specs=[pl.BlockSpec(memory_space=pltpu.SMEM)] + [whole] * (len(grads) + len(weights)),
        out_specs=[whole] * len(outs),
        compiler_params=pltpu.CompilerParams(vmem_limit_bytes=16 * MIB),
    )(place, *grads, *weights)


def slice_columns(weights):
    rows, parts, columns = weights.shape
    x_size = lax.axis_size("x")
    return weights.reshape(rows, parts, x_size, columns // x_size).transpose(2, 1, 0, 3)


def gather_weights(part, chunk, at_source):
    x_size, rows, columns = chunk.shape
    z_size = lax.axis_size("z")
    near = lax.ppermute(chunk, ("y", "mp"), [(1, 0), (2, 3), (0, 2), (3, 1)])
    far = lax.ppermute(chunk, ("y", "mp"), [(1, 2), (2, 1)])
    merged = jnp.stack([jnp.where(at_source, chunk, near), jnp.where(at_source, near, far)], 0)
    up = down = merged.reshape(2, x_size * rows, columns)
    pieces = [up]
    for step in range(1, z_size // 2):
        up, down = shift(up, "z", 1), shift(down, "z", -1)
        pieces += [up, down]
    return pieces + [shift(down, "z", -1) if part else shift(up, "z", 1)]


def sum_over_x(far_low, far_high, own, near_low, near_high, last_low, last_high):
    up, down = shift(far_low, "x", 1), shift(far_high, "x", -1)
    below_high, above_low = shift(near_high, "x", 1), shift(last_low, "x", -1)
    below_low = shift((near_low + up.astype(F32)).astype(BF), "x", 1)
    above_high = shift((last_high + down.astype(F32)).astype(BF), "x", -1)
    return own, below_low, below_high, above_low, above_high


def on_device(section_rows, norm_gains, proj_weights, section_cotan, enc_lengths, dec_segments):
    side = lax.axis_index("section")
    own_y, own_z, own_c = (lax.axis_index(a) for a in ("y", "z", "mp"))
    rows, cotan, weights = section_rows[0], section_cotan[0], proj_weights[0]
    place = jnp.stack([side, own_z, lax.axis_index("x")])
    wide_rows = rows.astype(F32)

    square = jnp.sum(wide_rows * wide_rows, -1, keepdims=True)
    other = shift(square, "mp", 1)
    slices = slice_columns(weights)
    chunks = lax.all_to_all(slices, "x", 0, 0, tiled=True)
    inverse, left = prepare(
        place, enc_lengths, dec_segments, rows, cotan, norm_gains, square, other, chunks
    )
    gathered = lax.all_gather(left, "x")
    pieces = [gather_weights(part, chunks[:, part], own_y == own_c) for part in range(2)]

    keep, recv, full = [], [], []
    for part in range(2):
        own, other, meta, *assembled = project(part, place, gathered, pieces[part])
        full += assembled
        other = shift(other, "mp", 1)

        def half(at):
            picked = [lax.dynamic_index_in_dim(whole, at, 0, False) for whole in (own, other)]
            return (picked[0] + picked[1].astype(F32)).astype(BF)

        recv.append(shift(half(1 - side), "section", 1))
        keep.append(half(side))
    stay, back = attention(place, meta, keep, recv)
    back = shift(back, "section", 1)
    grads = (stay, back, shift(stay, "mp", 1), shift(back, "mp", 1))
    row_count, half_width = rows.shape

    def outs(*kinds):
        return [jax.ShapeDtypeStruct((row_count // 2, half_width), kind) for kind in kinds]

    far = back_project((2,), outs(BF, BF), place, grads, full)
    whole = [jax.ShapeDtypeStruct(rows.shape, F32)]
    near = back_project((0, 1, 3), whole + outs(F32, BF, BF, F32), place, grads, full)
    parts = sum_over_x(*far, *near)
    gain_grad, row_dot = finish(place, rows, cotan, norm_gains, parts)
    row_dot = (row_dot + shift(row_dot, "mp", 1)) / (2 * rows.shape[1])
    result = inverse * gain_grad - wide_rows * inverse**3 * row_dot
    return (result + jnp.where(side == 0, 0.0, cotan.astype(F32)))[None]


def solution(mesh):
    names = ("section", "y", "x", "z", "mp")
    split = Mesh(mesh.devices.reshape(2, 2, 4, 8, 2), names)
    fsdp = ("y", "x", "z")
    return jax.shard_map(
        on_device,
        mesh=split,
        in_specs=(
            P("section", fsdp, "mp"),
            P("section", "mp"),
            P("section", fsdp, None, "mp"),
            P("section", fsdp, "mp"),
            P(fsdp, None),
            P(fsdp, None),
        ),
        out_specs=P("section", fsdp, "mp"),
        check_vma=False,
    )
```
